32 devices in a mesh: groups: 2 (over x), seq: 8 (over z, y), head: 2 (over core).
Axes of the slice: x: 2, y: 2, z: 4, core: 2. Of those that a mesh axis runs over, the one named last changes fastest.
Arguments:
- tokens: bfloat16 [8192, 3072], P(('groups', 'seq')), parts along dimension 0, may hold values from -6 to 6
- w_query: bfloat16 [32, 3072, 128], P('head', 'seq'), may hold values from -0.109375 to 0.109375
- w_key: bfloat16 [32, 3072, 128], P('head', 'seq'), may hold values from -0.109375 to 0.109375
- w_value: bfloat16 [32, 3072, 128], P('head', 'seq'), may hold values from -0.109375 to 0.109375
- norm_gain: float32 [32, 128], P('head'), may hold values from 0.25 to 1.75
- log_decay: bfloat16 [32, 8192], P('head', ('groups', 'seq')), parts along dimension 1, may hold values from -1 to 0
- lengths: int32 [8], P('groups'), parts along dimension 0, may hold values from 1 to 2048, 4096 in all
Outputs:
- output: bfloat16 [8192, 32, 128], P(('groups', 'seq'), 'head'), parts along dimension 0
The draws below stay inside these ranges and needn't reach their ends.
There are 2 independent parts, one for each index of `groups`. The reference program is written for one: setup_inputs(seed, part) draws one part's arguments, and reference() takes and returns one part's arrays. A program takes and returns all parts, laid end to end along the dimension named above; an argument that names none is the same for every part. Nothing has to cross between parts.
Inputs may be any that keep to these rules, and one draw needn't show every extreme that they name: The 4 lengths sum to 4096.
All inputs are finite; a program needn't handle non-finite values.
Results may differ from the reference program's by a relative error of at most 0.007.
Values may be sent and summed in bfloat16 or wider, within the bound.
A program may use at most 128 MiB of HBM per device.

```python
import math
import jax
import jax.numpy as jnp
import numpy as np
from jax import lax

D = 3072
HEAD_COUNT = 32
HD = 128
BLOCK = 128
PROMPTS = 4
TOK_DEV = 512
SLAB_TOKENS = 4096


def draw_log_decay(key, part):
    random_child_keys = jax.random.split(key, 7)
    ranking = jax.random.permutation(random_child_keys[0], HEAD_COUNT)
    slow_heads = ranking < HEAD_COUNT // 2
    fast_rates = jnp.exp(jax.random.uniform(random_child_keys[1], (HEAD_COUNT, 1), jnp.float32, math.log(1.0 / 50.0), math.log(1.0 / 30.0)))
    slow_rates = jax.random.uniform(random_child_keys[2], (HEAD_COUNT, 1), jnp.float32, 0.03, 0.1) * (math.log(10.0) / SLAB_TOKENS)
    rates = jnp.where(slow_heads[:, None], slow_rates, fast_rates)
    shards = SLAB_TOKENS // TOK_DEV
    factor = jnp.exp(jax.random.uniform(random_child_keys[3], (HEAD_COUNT, shards), jnp.float32, math.log(0.6), math.log(1.5)))
    factor = jnp.repeat(factor, TOK_DEV, axis=1)
    jitter = jax.random.uniform(random_child_keys[4], (HEAD_COUNT, SLAB_TOKENS), jnp.float32, 0.5, 1.5)
    spike_positions = jax.random.randint(random_child_keys[5], (HEAD_COUNT, 3), 0, SLAB_TOKENS)
    token_locations = jnp.arange(SLAB_TOKENS, dtype=jnp.int32)
    spike_decay_flag = jnp.any(token_locations[None, :, None] == spike_positions[:, None, :], axis=2)
    spike_decay_drop = jnp.log(jax.random.uniform(random_child_keys[6], (HEAD_COUNT, SLAB_TOKENS), jnp.float32, 0.5, 0.8))
    value_rows = -rates * factor * jitter
    return jnp.where(spike_decay_flag, value_rows + spike_decay_drop, value_rows).astype(jnp.bfloat16)


def steps_of(key, shape, cuts, low, top_value):
    def one(dim, parts):
        draws = jax.random.uniform(jax.random.fold_in(jax.random.fold_in(key, 6), dim), (parts,), jnp.float32, low / len(cuts), top_value / len(cuts))
        return jnp.repeat(jnp.exp(draws), shape[dim] // parts).reshape((-1,) + (1,) * (len(shape) - dim - 1))

    level = one(*cuts[0])
    for cut in cuts[1:]:
        level = level * one(*cut)
    return level


def split_up(count, total, most, lean):
    weights = [(1 << 20) // math.isqrt(rank ** lean) + 1 for rank in range(2, count + 1)]
    rest, given = total - most - (count - 1), [1] * (count - 1)
    while rest > 0:
        movable = [i for i in range(count - 1) if given[i] < most]
        mass, budget = sum([weights[i] for i in movable]), rest
        for i in movable:
            extra = min(most - given[i], max(1, budget * weights[i] // mass), rest)
            given[i] = given[i] + extra
            rest = rest - extra
    return np.array([most] + given)


def uneven_parts(key, amount, total, most, skew):
    if amount == 2:
        one = jax.random.randint(key, (), max(1, total - most), min(most, total - 1) + 1)
        return jnp.stack([one, total - one])
    tallies = jnp.asarray(split_up(amount, total, most, skew), jnp.int32)
    pairs = (amount - 1) // 2
    giver, taker = tallies[1:1 + 2 * pairs:2], tallies[2:2 + 2 * pairs:2]
    room = jnp.minimum(giver - 1, most - taker)
    moved = jax.random.randint(jax.random.fold_in(key, 1), (pairs,), 0, 1 << 20) % (room + 1)
    tallies = tallies.at[1:1 + 2 * pairs:2].set(giver - moved).at[2:2 + 2 * pairs:2].set(taker + moved)
    return tallies[jax.random.permutation(jax.random.fold_in(key, 2), amount)]


def bell_draw(own_key, dims, deviation, bound, cuts=(), kind=jnp.bfloat16):
    entries = jax.random.normal(own_key, dims, jnp.float32) * deviation
    if len(cuts) > 0:
        entries = steps_of(own_key, dims, cuts, -0.22, 0.18) * entries
    return jnp.clip(entries, min=-bound, max=bound).astype(kind)


def setup_inputs(seed: int = 0, part: int = 0) -> dict:
    key_of = jax.random.split(jax.random.key(seed), 8)
    part_splits = jax.random.split(jax.random.fold_in(key_of[7], part), 8)
    tokens = bell_draw(part_splits[0], (SLAB_TOKENS, D), 1.0, 6.0, ((0, 8),))
    w_query = bell_draw(key_of[1], (HEAD_COUNT, D, HD), D ** -0.5, 0.109375, ((0, 2), (1, 8)))
    w_key = bell_draw(key_of[2], (HEAD_COUNT, D, HD), D ** -0.5, 0.109375, ((0, 2), (1, 8)))
    w_value = bell_draw(key_of[3], (HEAD_COUNT, D, HD), D ** -0.5, 0.109375, ((0, 2), (1, 8)))
    norm_gain = jnp.clip(1.0 + 0.15 * jax.random.normal(key_of[4], (HEAD_COUNT, HD), jnp.float32), 0.25, 1.75)
    log_decay = draw_log_decay(jax.random.fold_in(jax.random.fold_in(key_of[7], part), 71), part)
    lengths = uneven_parts(part_splits[6], PROMPTS, SLAB_TOKENS, SLAB_TOKENS // 2, 2).astype(jnp.int32)
    return dict(tokens=tokens, w_query=w_query, w_key=w_key, w_value=w_value, norm_gain=norm_gain, log_decay=log_decay, lengths=lengths)


def segment_info(lengths, first_pos, rows_here):
    positions = first_pos + jnp.arange(rows_here, dtype=jnp.int32)
    prompt_ends = jnp.cumsum(lengths).astype(jnp.int32)
    prompt_begins = (prompt_ends - lengths).astype(jnp.int32)
    is_start = jnp.any(positions[:, None] == prompt_begins[None, :], axis=1)
    segment = lax.optimization_barrier(jnp.sum((positions[:, None] >= prompt_ends[None, :]).astype(jnp.int32), axis=1))
    return (is_start, segment)

def local_blocks(query, keys, value_rows, log_decay, is_start, segment, block_len):
    rows_here, heads_here, head_size = query.shape
    blocks = rows_here // block_len
    query_blk = query.reshape(blocks, block_len, heads_here, head_size).astype(jnp.float32)
    keys_blk = keys.reshape(blocks, block_len, heads_here, head_size)
    values_blk = value_rows.reshape(blocks, block_len, heads_here, head_size).astype(jnp.float32)
    running = jnp.cumsum(log_decay.astype(jnp.float32).reshape(heads_here, blocks, block_len), axis=2)
    starts_seen = jnp.cumsum(is_start.reshape(blocks, block_len).astype(jnp.int32), axis=1)
    started = starts_seen > 0
    later_start = starts_seen[:, -1:] - starts_seen > 0
    prompt_ids = segment.reshape(blocks, block_len)
    offsets = jnp.arange(block_len)
    visible = (offsets[:, None] >= offsets[None, :])[None] & (prompt_ids[:, :, None] == prompt_ids[:, None, :])
    gap_log = running[:, :, :, None] - running[:, :, None, :]
    decay_w = jnp.where(visible[None], jnp.exp(jnp.where(visible[None], gap_log, 0.0)), 0.0)
    scores = jnp.einsum('nthe,nshe->hnts', query_blk, keys_blk.astype(jnp.float32))
    weights_bf = (scores * decay_w).astype(jnp.bfloat16)
    intra = jnp.einsum('hnts,nshe->nthe', weights_bf.astype(jnp.float32), values_blk)
    carry_out = jnp.where(later_start[None], 0.0, jnp.exp(running[:, :, -1:] - running))
    weighted = (keys_blk * jnp.transpose(carry_out, (1, 2, 0))[..., None]).astype(jnp.bfloat16)
    block_update = jnp.einsum('nshd,nshe->nhde', weighted.astype(jnp.float32), values_blk)
    block_decay = jnp.where(started[:, -1][None], 0.0, jnp.exp(running[:, :, -1]))
    enter_decay = jnp.where(started[None], 0.0, jnp.exp(running))
    return (intra, enter_decay, block_update, block_decay)

def block_states(block_update, block_decay):

    def advance(carried_in, inputs):
        current, product = carried_in
        one_update, one_decay = inputs
        return ((one_decay[:, None, None] * current + one_update, product * one_decay), (current, product))
    initial = (jnp.zeros(block_update.shape[1:], jnp.float32), jnp.ones((block_decay.shape[0],), jnp.float32))
    outcome, history = lax.scan(advance, initial, (block_update, jnp.transpose(block_decay)))
    return history[0]

def reference(tokens, w_query, w_key, w_value, norm_gain, log_decay, lengths):
    tokens_wide = tokens.astype(jnp.float32)
    query = jnp.einsum('td,hde->the', tokens_wide, w_query.astype(jnp.float32)).astype(jnp.bfloat16)
    keys = jnp.einsum('td,hde->the', tokens_wide, w_key.astype(jnp.float32)).astype(jnp.bfloat16)
    value_rows = jnp.einsum('td,hde->the', tokens_wide, w_value.astype(jnp.float32)).astype(jnp.bfloat16)
    rows_all, heads_all, head_size = query.shape
    block_len = BLOCK
    is_start, segment = segment_info(lengths, 0, rows_all)
    intra, enter_decay, block_update, block_decay = local_blocks(query, keys, value_rows, log_decay, is_start, segment, block_len)
    states = block_states(block_update, block_decay)
    states_bf = states.astype(jnp.bfloat16).astype(jnp.float32)
    blocks = rows_all // block_len
    query_blk = query.reshape(blocks, block_len, heads_all, head_size).astype(jnp.float32)
    carried = jnp.einsum('nthe,nhef->nthf', query_blk, states_bf)
    attended = intra + carried * jnp.transpose(enter_decay, (1, 2, 0))[..., None]
    inv_rms = lax.rsqrt(lax.optimization_barrier(jnp.mean(attended * attended, axis=-1, keepdims=True)) + 1e-06)
    result = (attended * inv_rms * norm_gain[None, None, :, :]).astype(jnp.bfloat16)
    return result.reshape(rows_all, heads_all, head_size)
```

```python
import functools

import jax
import jax.numpy as jnp
from jax import lax
from jax.experimental import pallas as pl
from jax.experimental.pallas import tpu as pltpu
from jax.sharding import PartitionSpec as P

BLOCK = 128
NT = (((1,), (1,)), ((), ()))
TN = (((0,), (0,)), ((), ()))
F32 = jnp.float32
BF16 = jnp.bfloat16


def attend_block(q, k, v, decay, seg, state, gain, consts):
    lower, upper, above = consts
    visible, entered, leaves, passes = seg
    size = q.shape[0]
    rows = jnp.broadcast_to(decay, (size, size))
    gap = lax.dot_general(lower, jnp.where(above, rows, 0), NT, preferred_element_type=F32)
    running = lax.dot_general(lower, rows, NT, preferred_element_type=F32)
    rest = lax.dot_general(upper, rows, NT, preferred_element_type=F32)
    scores = lax.dot_general(q, k, NT, preferred_element_type=F32)
    weights = (scores * jnp.where(visible, jnp.exp(gap), 0.0)).astype(BF16)
    intra = jnp.dot(weights, v, preferred_element_type=F32)
    enter = jnp.where(entered, 0.0, jnp.exp(running))
    carried = jnp.dot(q, state.astype(BF16), preferred_element_type=F32)
    attended = intra + enter * carried
    inv = lax.rsqrt(jnp.mean(attended * attended, axis=1, keepdims=True) + 1e-06)
    out = (attended * inv * gain).astype(BF16)
    carry = jnp.where(leaves, 0.0, jnp.exp(rest))
    weighted = (k.astype(F32) * carry).astype(BF16)
    update = lax.dot_general(weighted, v, TN, preferred_element_type=F32)
    keep = jnp.where(passes, jnp.exp(running[size - 1 : size, :]), 0.0)
    return out, keep * state + update


def segment_of(position, lens_ref, base, prompts):
    end = jnp.int32(0)
    total = 0 * position
    for j in range(prompts):
        end = end + lens_ref[base + j]
        total = total + jnp.where(position >= end, 1, 0)
    return total


def kernel(prompts, lens_ref, tok_ref, w_ref, ld_ref, gain_ref, out_ref, state_ref):
    step = pl.program_id(0)
    heads = ld_ref.shape[0]
    rows = tok_ref.shape[0]
    size = gain_ref.shape[1]

    @pl.when(step == 0)
    def _():
        state_ref[...] = jnp.zeros_like(state_ref)

    qkv = jnp.dot(tok_ref[...], w_ref[...], preferred_element_type=F32).astype(BF16)
    ti = lax.broadcasted_iota(jnp.int32, (BLOCK, BLOCK), 0)
    si = lax.broadcasted_iota(jnp.int32, (BLOCK, BLOCK), 1)
    consts = ((ti >= si).astype(F32).astype(BF16), (ti < si).astype(F32).astype(BF16), ti < si)
    for b in range(rows // BLOCK):
        first = (step * rows + b * BLOCK).astype(jnp.int32)
        seg_t = segment_of(first + ti, lens_ref, 0, prompts)
        seg_s = segment_of(first + si, lens_ref, 0, prompts)
        seg_before = segment_of(first - 1, lens_ref, 0, prompts)
        seg_last = segment_of(first + BLOCK - 1, lens_ref, 0, prompts)
        seg_before = jnp.where(first == 0, -1, seg_before)
        seg = (
            (ti >= si) & (seg_t == seg_s),
            seg_t != seg_before,
            seg_t != seg_last,
            seg_before == seg_last,
        )
        here = slice(b * BLOCK, (b + 1) * BLOCK)
        for h in range(heads):
            part = [qkv[here, (i * heads + h) * size : (i * heads + h + 1) * size] for i in range(3)]
            out, state = attend_block(
                *part, ld_ref[h : h + 1, here], seg, state_ref[h], gain_ref[h : h + 1, :], consts
            )
            state_ref[h] = state
            out_ref[here, h * size : (h + 1) * size] = out


def body(tokens, w_query, w_key, w_value, norm_gain, log_decay, lengths):
    rows_here, width = tokens.shape
    heads_here, depth, size = w_query.shape
    count = lax.axis_size("seq")
    mine = heads_here // count
    cores = lax.axis_size("head")
    part = width // cores
    half = lax.dynamic_slice(tokens, (0, lax.axis_index("head") * part), (rows_here, part))
    gathered = lax.all_gather(half, "seq", axis=0, tiled=True)
    everyone = lax.all_gather(gathered, "head", axis=1, tiled=True)
    stacked = jnp.stack([w_query, w_key, w_value])
    moved = lax.all_to_all(stacked, "seq", split_axis=1, concat_axis=2, tiled=True)
    weights = jnp.transpose(moved, (2, 0, 1, 3)).reshape(width, 3 * mine * size)
    decays = lax.all_gather(log_decay, "seq", axis=1, tiled=True)
    first_head = lax.axis_index("seq") * mine
    decays = lax.dynamic_slice_in_dim(decays, first_head, mine, axis=0)
    gains = lax.dynamic_slice_in_dim(norm_gain, first_head, mine, axis=0)
    total = rows_here * count
    out = pl.pallas_call(
        functools.partial(kernel, lengths.shape[0]),
        grid=(count,),
        out_shape=jax.ShapeDtypeStruct((total, mine * size), BF16),
        in_specs=[
            pl.BlockSpec(memory_space=pltpu.SMEM),
            pl.BlockSpec((rows_here, width), lambda i: (i, 0)),
            pl.BlockSpec((width, 3 * mine * size), lambda i: (0, 0)),
            pl.BlockSpec((mine, rows_here), lambda i: (0, i)),
            pl.BlockSpec((mine, size), lambda i: (0, 0)),
        ],
        out_specs=pl.BlockSpec((rows_here, mine * size), lambda i: (i, 0)),
        scratch_shapes=[pltpu.VMEM((mine, size, size), F32)],
        compiler_params=pltpu.CompilerParams(vmem_limit_bytes=48 * 2**20),
    )(lengths, everyone, weights, decays, gains)
    back = lax.all_to_all(out, "seq", split_axis=0, concat_axis=1, tiled=True)
    return back.reshape(rows_here, heads_here, size)


def solution(mesh):
    return jax.shard_map(
        body,
        mesh=mesh,
        in_specs=(
            P(("groups", "seq"), None),
            P("head", "seq", None),
            P("head", "seq", None),
            P("head", "seq", None),
            P("head", None),
            P("head", ("groups", "seq")),
            P("groups"),
        ),
        out_specs=P(("groups", "seq"), "head", None),
        check_vma=False,
    )
```

```python
import functools

import jax
import jax.numpy as jnp
from jax import lax
from jax.experimental import pallas as pl
from jax.experimental.pallas import tpu as pltpu
from jax.sharding import PartitionSpec as P

BLOCK = 128
NT = (((1,), (1,)), ((), ()))
TN = (((0,), (0,)), ((), ()))
F32 = jnp.float32
BF16 = jnp.bfloat16
MESH = pl.DeviceIdType.MESH


def attend_block(q, k, v, decay, seg, state, gain, consts):
    lower, upper, above = consts
    visible, entered, leaves, passes = seg
    size = q.shape[0]
    rows = jnp.broadcast_to(decay, (size, size))
    gap = lax.dot_general(lower, jnp.where(above, rows, 0), NT, preferred_element_type=F32)
    running = lax.dot_general(lower, rows, NT, preferred_element_type=F32)
    rest = lax.dot_general(upper, rows, NT, preferred_element_type=F32)
    scores = lax.dot_general(q, k, NT, preferred_element_type=F32)
    weights = (scores * jnp.where(visible, jnp.exp(gap), 0.0)).astype(BF16)
    intra = jnp.dot(weights, v, preferred_element_type=F32)
    enter = jnp.where(entered, 0.0, jnp.exp(running))
    carried = jnp.dot(q, state.astype(BF16), preferred_element_type=F32)
    attended = intra + enter * carried
    inv = lax.rsqrt(jnp.mean(attended * attended, axis=1, keepdims=True) + 1e-06)
    out = (attended * inv * gain).astype(BF16)
    carry = jnp.where(leaves, 0.0, jnp.exp(rest))
    weighted = (k.astype(F32) * carry).astype(BF16)
    update = lax.dot_general(weighted, v, TN, preferred_element_type=F32)
    keep = jnp.where(passes, jnp.exp(running[size - 1 : size, :]), 0.0)
    return out, keep * state + update


def segment_of(position, lens_ref, base, prompts):
    end = jnp.int32(0)
    total = 0 * position
    for j in range(prompts):
        end = end + lens_ref[base + j]
        total = total + jnp.where(position >= end, 1, 0)
    return total


def attend_kernel(prompts, lens_ref, qkv_ref, ld_ref, gain_ref, out_ref, state_ref):
    step = pl.program_id(0)
    heads = ld_ref.shape[0]
    rows = qkv_ref.shape[0]
    size = gain_ref.shape[1]

    @pl.when(step == 0)
    def _():
        state_ref[...] = jnp.zeros_like(state_ref)

    ti = lax.broadcasted_iota(jnp.int32, (BLOCK, BLOCK), 0)
    si = lax.broadcasted_iota(jnp.int32, (BLOCK, BLOCK), 1)
    consts = ((ti >= si).astype(F32).astype(BF16), (ti < si).astype(F32).astype(BF16), ti < si)
    for b in range(rows // BLOCK):
        first = (step * rows + b * BLOCK).astype(jnp.int32)
        seg_t = segment_of(first + ti, lens_ref, 0, prompts)
        seg_s = segment_of(first + si, lens_ref, 0, prompts)
        seg_before = segment_of(first - 1, lens_ref, 0, prompts)
        seg_last = segment_of(first + BLOCK - 1, lens_ref, 0, prompts)
        seg_before = jnp.where(first == 0, -1, seg_before)
        seg = (
            (ti >= si) & (seg_t == seg_s),
            seg_t != seg_before,
            seg_t != seg_last,
            seg_before == seg_last,
        )
        here = slice(b * BLOCK, (b + 1) * BLOCK)
        for h in range(heads):
            part = [qkv_ref[here, (i * heads + h) * size : (i * heads + h + 1) * size] for i in range(3)]
            out, state = attend_block(
                *part, ld_ref[h : h + 1, here], seg, state_ref[h], gain_ref[h : h + 1, :], consts
            )
            state_ref[h] = state
            out_ref[here, h * size : (h + 1) * size] = out


def gather_kernel(
    inner, tok_hbm, wq, wk, wv, out_ref, tok, landed, joined,
    own_sem, w_own, z_send, y_send, core_send, tok_recv, w_send, w_recv,
):
    count = lax.axis_size("seq")
    outer = count // inner
    me, core, group = lax.axis_index("seq"), lax.axis_index("head"), lax.axis_index("groups")
    far, near = me // inner, me % inner
    weights = (wq, wk, wv)
    mine, depth = wq.shape[0] // count, wq.shape[1]
    part = depth // 2
    side = group % 2
    rows = tok.shape[2]
    size = wq.shape[2]
    other_core = {"head": 1 - core}
    twin = {"groups": group + 1 - 2 * side}

    barrier = pltpu.get_barrier_semaphore()
    for i in range(1, count):
        pl.semaphore_signal(barrier, device_id={"seq": (me + i) % count}, device_id_type=MESH)
    pl.semaphore_signal(barrier, device_id=other_core, device_id_type=MESH)
    pl.semaphore_signal(barrier, device_id=twin, device_id_type=MESH)
    pl.semaphore_wait(barrier, count + 1)

    def own_copy(h):
        return pltpu.make_async_copy(tok_hbm.at[pl.ds(h * rows, rows)], tok.at[me, h], own_sem.at[h])

    def own_weights(m):
        return pltpu.make_async_copy(
            weights[m].at[pl.ds(me * mine, mine)],
            landed.at[m, :, pl.ds(pl.multiple_of(me * depth, 16), depth)],
            w_own.at[m],
        )

    def remote(src, dst, send, recv, device):
        return pltpu.make_async_remote_copy(
            src_ref=src, dst_ref=dst, send_sem=send, recv_sem=recv, device_id=device, device_id_type=MESH
        )

    def shard(s, h, send, device):
        return remote(tok.at[s, h], tok.at[s, h], send, tok_recv.at[s, h], device)

    def slot(m, s, half):
        start = pl.multiple_of(s * depth + half * part, 16)
        return landed.at[m, :, pl.ds(start, part)]

    def weight_out(m, i):
        to = (me + i) % count
        src = weights[m].at[pl.ds(to * mine, mine), pl.ds(pl.multiple_of(side * part, 16), part)]
        return remote(src, slot(m, me, side), w_send.at[0, i, m], w_recv.at[side, me, m], {"seq": to})

    def weight_over(m, i):
        s = (me + count - i) % count
        return remote(slot(m, s, side), slot(m, s, side), w_send.at[1, i, m], w_recv.at[side, s, m], twin)

    def weight_in(m, i, half):
        s = (me + count - i) % count
        return remote(slot(m, s, half), slot(m, s, half), w_send.at[1, i, m], w_recv.at[half, s, m], twin)

    for h in range(2):
        own_copy(h).start()
    for m in range(3):
        own_weights(m).start()
    for h in range(2):
        own_copy(h).wait()

    def forwards(j, act):
        step = (j + 1) // 2
        offset = jnp.where(j % 2 == 1, -step, step)
        place = far + offset
        s = place * inner + near
        inside = (place >= 0) & (place < outer)

        @pl.when(inside & (offset <= 0) & (far + 1 < outer))
        def _():
            act(shard(s, core, z_send.at[0, j], {"seq": me + inner}))

        @pl.when(inside & (offset >= 0) & (far > 0))
        def _():
            act(shard(s, core, z_send.at[1, j], {"seq": me - inner}))

        for k in range(1, inner):
            @pl.when(inside)
            def _():
                act(shard(s, core, y_send.at[k, j], {"seq": far * inner + (near + k) % inner}))

        @pl.when(inside & (j > 0))
        def _():
            act(shard(s, core, core_send.at[0, j], other_core))

    def crossing(j, act):
        step = (j + 1) // 2
        place = far + jnp.where(j % 2 == 1, -step, step)
        for k in range(1, inner):
            s = place * inner + (near + k) % inner

            @pl.when((place >= 0) & (place < outer))
            def _():
                act(shard(s, core, core_send.at[k, j], other_core), s)

    def arrived(s, h):
        shard(s, h, own_sem.at[0], other_core).wait_recv()

    def receive_and_start(copy, s):
        arrived(s, core)
        copy.start()

    forwards(0, lambda copy: copy.start())
    for i in range(1, count):
        for m in range(3):
            weight_out(m, i).start()

    last = 2 * outer - 1

    def serve(j, carry):
        step = (j + 1) // 2
        place = far + jnp.where(j % 2 == 1, -step, step)

        @pl.when((j < last) & (place >= 0) & (place < outer))
        def _():
            arrived(place * inner + near, core)

        @pl.when(j < last)
        def _():
            forwards(j, lambda copy: copy.start())

        @pl.when(j >= 2)
        def _():
            crossing(j - 2, receive_and_start)

        for k in range(2):
            i = 2 * (j - 3) + 1 + k

            @pl.when((i >= 1) & (i < count))
            def _():
                for m in range(3):
                    weight_in(m, i, side).wait_recv()
                    weight_over(m, i).start()

        return carry

    lax.fori_loop(1, last + 2, serve, 0)

    for m in range(3):
        own_weights(m).wait()
    for i in range(1, count):
        for m in range(3):
            weight_in(m, i, 1 - side).wait_recv()

    def join(s, carry):
        here = pl.ds(pl.multiple_of(s * depth, 16), depth)
        for m in range(3):
            for h in range(mine):
                at = (m * mine + h) * size
                joined[here, at : at + size] = landed[m, h, here, :]
        return carry

    lax.fori_loop(0, count, join, 0)

    def project(i, carry):
        s = (me + i) % count

        @pl.when(i > 0)
        def _():
            arrived(s, 1 - core)

        for h in range(2):
            start = pl.multiple_of((2 * s + h) * rows, 16)
            out_ref[pl.ds(start, rows), :] = jnp.dot(
                tok[s, h], joined[...], preferred_element_type=F32
            ).astype(BF16)
        return carry

    lax.fori_loop(0, count, project, 0)

    def drain(j, carry):
        forwards(j, lambda copy: copy.wait_send())
        crossing(j, lambda copy, s: copy.wait_send())
        return carry

    lax.fori_loop(0, last, drain, 0)
    for i in range(1, count):
        for m in range(3):
            weight_out(m, i).wait_send()
            weight_over(m, i).wait_send()


def project_remote(inner, tokens, w_query, w_key, w_value):
    rows_here, width = tokens.shape
    heads_here, depth, size = w_query.shape
    count = lax.axis_size("seq")
    mine = heads_here // count
    outer = count // inner
    columns = 3 * mine * size
    anywhere = pl.BlockSpec(memory_space=pl.ANY)
    dma = pltpu.SemaphoreType.DMA
    return pl.pallas_call(
        functools.partial(gather_kernel, inner),
        out_shape=jax.ShapeDtypeStruct((rows_here * count, columns), BF16),
        in_specs=[anywhere] * 4,
        out_specs=pl.BlockSpec(memory_space=pltpu.VMEM),
        scratch_shapes=[
            pltpu.VMEM((count, 2, rows_here // 2, width), BF16),
            pltpu.VMEM((3, mine, width, size), BF16),
            pltpu.VMEM((width, columns), BF16),
            dma((2,)),
            dma((3,)),
            dma((2, 2 * outer)),
            dma((inner, 2 * outer)),
            dma((inner, 2 * outer)),
            dma((count, 2)),
            dma((2, count, 3)),
            dma((2, count, 3)),
        ],
        compiler_params=pltpu.CompilerParams(
            collective_id=0, has_side_effects=True, vmem_limit_bytes=56 * 2**20
        ),
    )(tokens, w_query, w_key, w_value)


def project_plain(tokens, w_query, w_key, w_value):
    rows_here, width = tokens.shape
    heads_here, depth, size = w_query.shape
    mine = heads_here // lax.axis_size("seq")
    part = width // lax.axis_size("head")
    half = lax.dynamic_slice(tokens, (0, lax.axis_index("head") * part), (rows_here, part))
    gathered = lax.all_gather(half, "seq", axis=0, tiled=True)
    everyone = lax.all_gather(gathered, "head", axis=1, tiled=True)
    stacked = jnp.stack([w_query, w_key, w_value])
    moved = lax.all_to_all(stacked, "seq", split_axis=1, concat_axis=2, tiled=True)
    weights = jnp.transpose(moved, (2, 0, 1, 3)).reshape(width, 3 * mine * size)
    return jnp.dot(everyone, weights, preferred_element_type=F32).astype(BF16)


def body(tokens, w_query, w_key, w_value, norm_gain, log_decay, lengths):
    rows_here, width = tokens.shape
    heads_here, depth, size = w_query.shape
    count = lax.axis_size("seq")
    mine = heads_here // count
    total = rows_here * count
    fits = 2 * (total * width + total * 3 * mine * size + 6 * mine * size * width) < 48 * 2**20
    if fits and lax.axis_size("groups") % 2 == 0 and lax.axis_size("head") == 2:
        inner = 2 if count % 2 == 0 else 1
        qkv = project_remote(inner, tokens, w_query, w_key, w_value)
    else:
        qkv = project_plain(tokens, w_query, w_key, w_value)
    decays = lax.all_gather(log_decay, "seq", axis=1, tiled=True)
    first_head = lax.axis_index("seq") * mine
    decays = lax.dynamic_slice_in_dim(decays, first_head, mine, axis=0)
    gains = lax.dynamic_slice_in_dim(norm_gain, first_head, mine, axis=0)
    out = pl.pallas_call(
        functools.partial(attend_kernel, lengths.shape[0]),
        grid=(count,),
        out_shape=jax.ShapeDtypeStruct((total, mine * size), BF16),
        in_specs=[
            pl.BlockSpec(memory_space=pltpu.SMEM),
            pl.BlockSpec((rows_here, 3 * mine * size), lambda i: (i, 0)),
            pl.BlockSpec((mine, rows_here), lambda i: (0, i)),
            pl.BlockSpec((mine, size), lambda i: (0, 0)),
        ],
        out_specs=pl.BlockSpec((rows_here, mine * size), lambda i: (i, 0)),
        scratch_shapes=[pltpu.VMEM((mine, size, size), F32)],
        compiler_params=pltpu.CompilerParams(vmem_limit_bytes=32 * 2**20),
    )(lengths, qkv, decays, gains)
    back = lax.all_to_all(out, "seq", split_axis=0, concat_axis=1, tiled=True)
    return back.reshape(rows_here, heads_here, size)


def solution(mesh):
    return jax.shard_map(
        body,
        mesh=mesh,
        in_specs=(
            P(("groups", "seq"), None),
            P("head", "seq", None),
            P("head", "seq", None),
            P("head", "seq", None),
            P("head", None),
            P("head", ("groups", "seq")),
            P("groups"),
        ),
        out_specs=P(("groups", "seq"), "head", None),
        check_vma=False,
    )
```

```python
import functools

import jax
import jax.numpy as jnp
from jax import lax
from jax.experimental import pallas as pl
from jax.experimental.pallas import tpu as pltpu
from jax.sharding import PartitionSpec as P

BLOCK = 128
NT = (((1,), (1,)), ((), ()))
TN = (((0,), (0,)), ((), ()))
F32 = jnp.float32
BF16 = jnp.bfloat16
MESH = pl.DeviceIdType.MESH


def attend_block(q, k, v, decay, seg, state, gain, consts):
    lower, upper, above = consts
    visible, entered, leaves, passes = seg
    size = q.shape[0]
    rows = jnp.broadcast_to(decay, (size, size))
    gap = lax.dot_general(lower, jnp.where(above, rows, 0), NT, preferred_element_type=F32)
    running = lax.dot_general(lower, rows, NT, preferred_element_type=F32)
    rest = lax.dot_general(upper, rows, NT, preferred_element_type=F32)
    scores = lax.dot_general(q, k, NT, preferred_element_type=F32)
    weights = (scores * jnp.where(visible, jnp.exp(gap), 0.0)).astype(BF16)
    intra = jnp.dot(weights, v, preferred_element_type=F32)
    enter = jnp.where(entered, 0.0, jnp.exp(running))
    carried = jnp.dot(q, state.astype(BF16), preferred_element_type=F32)
    attended = intra + enter * carried
    inv = lax.rsqrt(jnp.mean(attended * attended, axis=1, keepdims=True) + 1e-06)
    out = (attended * inv * gain).astype(BF16)
    carry = jnp.where(leaves, 0.0, jnp.exp(rest))
    weighted = (k.astype(F32) * carry).astype(BF16)
    update = lax.dot_general(weighted, v, TN, preferred_element_type=F32)
    keep = jnp.where(passes, jnp.exp(running[size - 1 : size, :]), 0.0)
    return out, keep * state + update


def segment_of(position, lens_ref, base, prompts):
    end = jnp.int32(0)
    total = 0 * position
    for j in range(prompts):
        end = end + lens_ref[base + j]
        total = total + jnp.where(position >= end, 1, 0)
    return total


def attend_shard(step, rows, heads, lens_ref, prompts, part, decay, gain, state_ref, store):
    ti = lax.broadcasted_iota(jnp.int32, (BLOCK, BLOCK), 0)
    si = lax.broadcasted_iota(jnp.int32, (BLOCK, BLOCK), 1)
    consts = ((ti >= si).astype(F32).astype(BF16), (ti < si).astype(F32).astype(BF16), ti < si)
    for b in range(rows // BLOCK):
        first = (step * rows + b * BLOCK).astype(jnp.int32)
        seg_t = segment_of(first + ti, lens_ref, 0, prompts)
        seg_s = segment_of(first + si, lens_ref, 0, prompts)
        seg_before = segment_of(first - 1, lens_ref, 0, prompts)
        seg_last = segment_of(first + BLOCK - 1, lens_ref, 0, prompts)
        seg_before = jnp.where(first == 0, -1, seg_before)
        seg = (
            (ti >= si) & (seg_t == seg_s),
            seg_t != seg_before,
            seg_t != seg_last,
            seg_before == seg_last,
        )
        for h in range(heads):
            out, state = attend_block(
                *part(b, h), decay(b, h), seg, state_ref[h], gain(h), consts
            )
            state_ref[h] = state
            store(b, h, out)


def attend_kernel(prompts, lens_ref, qkv_ref, ld_ref, gain_ref, out_ref, state_ref):
    step = pl.program_id(0)
    heads = ld_ref.shape[0]
    size = gain_ref.shape[1]

    @pl.when(step == 0)
    def _():
        state_ref[...] = jnp.zeros_like(state_ref)

    def here(b):
        return slice(b * BLOCK, (b + 1) * BLOCK)

    def part(b, h):
        return [qkv_ref[here(b), (i * heads + h) * size : (i * heads + h + 1) * size] for i in range(3)]

    def store(b, h, out):
        out_ref[here(b), h * size : (h + 1) * size] = out

    attend_shard(
        step, qkv_ref.shape[0], heads, lens_ref, prompts, part,
        lambda b, h: ld_ref[h : h + 1, here(b)], lambda h: gain_ref[h : h + 1, :], state_ref, store,
    )


def gather_kernel(
    inner, prompts, lens_ref, tok_hbm, wq, wk, wv, ld_ref, gain_ref, out_hbm,
    tok, landed, joined, qkv, ready, decays, wide, state_ref,
    own_sem, w_own, z_send, y_send, core_send, tok_recv, w_send, w_recv, d_send, d_recv, o_send, o_recv,
):
    count = lax.axis_size("seq")
    outer = count // inner
    me, core, group = lax.axis_index("seq"), lax.axis_index("head"), lax.axis_index("groups")
    far, near = me // inner, me % inner
    weights = (wq, wk, wv)
    mine, depth = wq.shape[0] // count, wq.shape[1]
    part = depth // 2
    side = group % 2
    rows = tok.shape[2]
    size = wq.shape[2]
    other_core = {"head": 1 - core}
    twin = {"groups": group + 1 - 2 * side}

    barrier = pltpu.get_barrier_semaphore()
    for i in range(1, count):
        pl.semaphore_signal(barrier, device_id={"seq": (me + i) % count}, device_id_type=MESH)
    pl.semaphore_signal(barrier, device_id=other_core, device_id_type=MESH)
    pl.semaphore_signal(barrier, device_id=twin, device_id_type=MESH)
    pl.semaphore_wait(barrier, count + 1)

    def own_copy(h):
        return pltpu.make_async_copy(tok_hbm.at[pl.ds(h * rows, rows)], tok.at[me, h], own_sem.at[h])

    def own_weights(m):
        return pltpu.make_async_copy(
            weights[m].at[pl.ds(me * mine, mine)],
            landed.at[m, :, pl.ds(pl.multiple_of(me * depth, 16), depth)],
            w_own.at[m],
        )

    def remote(src, dst, send, recv, device):
        return pltpu.make_async_remote_copy(
            src_ref=src, dst_ref=dst, send_sem=send, recv_sem=recv, device_id=device, device_id_type=MESH
        )

    def shard(s, h, send, device):
        return remote(tok.at[s, h], tok.at[s, h], send, tok_recv.at[s, h], device)

    def slot(m, s, half):
        start = pl.multiple_of(s * depth + half * part, 16)
        return landed.at[m, :, pl.ds(start, part)]

    def weight_out(m, i):
        to = (me + i) % count
        src = weights[m].at[pl.ds(to * mine, mine), pl.ds(pl.multiple_of(side * part, 16), part)]
        return remote(src, slot(m, me, side), w_send.at[0, i, m], w_recv.at[side, me, m], {"seq": to})

    def weight_over(m, i):
        s = (me + count - i) % count
        return remote(slot(m, s, side), slot(m, s, side), w_send.at[1, i, m], w_recv.at[side, s, m], twin)

    def weight_in(m, i, half):
        s = (me + count - i) % count
        return remote(slot(m, s, half), slot(m, s, half), w_send.at[1, i, m], w_recv.at[half, s, m], twin)

    def decay_copy(i):
        src = decays.at[me]
        return remote(src, src, d_send.at[i], d_recv.at[me], {"seq": (me + i) % count})

    def decay_in(i):
        s = (me + i) % count
        return remote(decays.at[s], decays.at[s], d_send.at[i], d_recv.at[s], {"seq": s})

    def columns_of(s):
        return pl.ds(pl.multiple_of(s * (mine * size), 128), mine * size)

    def result(s):
        return remote(ready.at[s], out_hbm.at[:, columns_of(me)], o_send.at[s], o_recv.at[me], {"seq": s})

    def result_in(i):
        s = (me + i) % count
        return remote(ready.at[s], out_hbm.at[:, columns_of(s)], o_send.at[s], o_recv.at[s], {"seq": s})

    def own_result():
        return pltpu.make_async_copy(ready.at[me], out_hbm.at[:, columns_of(me)], o_recv.at[me])

    for h in range(2):
        own_copy(h).start()
    decays[me] = ld_ref[...]
    for m in range(3):
        own_weights(m).start()
    for h in range(2):
        own_copy(h).wait()

    def forwards(j, act):
        step = (j + 1) // 2
        offset = jnp.where(j % 2 == 1, -step, step)
        place = far + offset
        s = place * inner + near
        inside = (place >= 0) & (place < outer)

        @pl.when(inside & (offset <= 0) & (far + 1 < outer))
        def _():
            act(shard(s, core, z_send.at[0, j], {"seq": me + inner}))

        @pl.when(inside & (offset >= 0) & (far > 0))
        def _():
            act(shard(s, core, z_send.at[1, j], {"seq": me - inner}))

        for k in range(1, inner):
            @pl.when(inside)
            def _():
                act(shard(s, core, y_send.at[k, j], {"seq": far * inner + (near + k) % inner}))

        @pl.when(inside & (j > 0))
        def _():
            act(shard(s, core, core_send.at[0, j], other_core))

    def crossing(j, act):
        step = (j + 1) // 2
        place = far + jnp.where(j % 2 == 1, -step, step)
        for k in range(1, inner):
            s = place * inner + (near + k) % inner

            @pl.when((place >= 0) & (place < outer))
            def _():
                act(shard(s, core, core_send.at[k, j], other_core), s)

    def arrived(s, h):
        shard(s, h, own_sem.at[0], other_core).wait_recv()

    def receive_and_start(copy, s):
        arrived(s, core)
        copy.start()

    forwards(0, lambda copy: copy.start())
    for i in range(1, count):
        for m in range(3):
            weight_out(m, i).start()
    for i in range(1, count):
        decay_copy(i).start()

    last = 2 * outer - 1

    def serve(j, carry):
        step = (j + 1) // 2
        place = far + jnp.where(j % 2 == 1, -step, step)

        @pl.when((j < last) & (place >= 0) & (place < outer))
        def _():
            arrived(place * inner + near, core)

        @pl.when(j < last)
        def _():
            forwards(j, lambda copy: copy.start())

        @pl.when(j >= 2)
        def _():
            crossing(j - 2, receive_and_start)

        for k in range(4):
            i = 4 * (j - 3) + 1 + k

            @pl.when((i >= 1) & (i < count))
            def _():
                for m in range(3):
                    weight_in(m, i, side).wait_recv()
                    weight_over(m, i).start()

        return carry

    lax.fori_loop(1, last, serve, 0)

    for m in range(3):
        own_weights(m).wait()
    for i in range(1, count):
        for m in range(3):
            weight_in(m, i, 1 - side).wait_recv()

    def join(s, carry):
        here = pl.ds(pl.multiple_of(s * depth, 16), depth)
        for m in range(3):
            for h in range(mine):
                at = (m * mine + h) * size
                joined[here, at : at + size] = landed[m, h, here, :]
        return carry

    lax.fori_loop(0, count, join, 0)

    def project(j, carry):
        step = (j + 1) // 2
        place = far + jnp.where(j % 2 == 1, -step, step)

        @pl.when((j >= last - 2) & (place >= 0) & (place < outer))
        def _():
            for k in range(1, inner):
                s = place * inner + (near + k) % inner
                receive_and_start(shard(s, core, core_send.at[k, j], other_core), s)

        @pl.when((place >= 0) & (place < outer))
        def _():
            def one(k, carry):
                s = place * inner + (near + k) % inner

                @pl.when(s != me)
                def _():
                    arrived(s, 1 - core)

                for h in range(2):
                    start = pl.multiple_of((2 * s + h) * rows, 16)
                    qkv[pl.ds(start, rows), :] = jnp.dot(
                        tok[s, h], joined[...], preferred_element_type=F32
                    ).astype(BF16)
                return carry

            lax.fori_loop(0, inner, one, 0)

        return carry

    lax.fori_loop(0, last, project, 0)

    for i in range(1, count):
        decay_in(i).wait_recv()
    for b in range(wide.shape[1]):
        wide[:, b] = decays[:, :, b * BLOCK : (b + 1) * BLOCK].astype(F32)
    state_ref[...] = jnp.zeros_like(state_ref)
    row_count = 2 * rows

    def attend(s, carry):
        def part(b, h):
            here = pl.ds(pl.multiple_of(s * row_count + b * BLOCK, BLOCK), BLOCK)
            return [qkv[here, (i * mine + h) * size : (i * mine + h + 1) * size] for i in range(3)]

        def decay(b, h):
            return wide[s, b, pl.ds(me * mine + h, 1), :].astype(BF16)

        def store(b, h, out):
            ready[s, b * BLOCK : (b + 1) * BLOCK, h * size : (h + 1) * size] = out

        attend_shard(
            s, row_count, mine, lens_ref, prompts, part, decay,
            lambda h: gain_ref[pl.ds(me * mine + h, 1), :], state_ref, store,
        )

        @pl.when(s != me)
        def _():
            result(s).start()

        @pl.when(s == me)
        def _():
            own_result().start()

        return carry

    lax.fori_loop(0, count, attend, 0)

    def drain(j, carry):
        forwards(j, lambda copy: copy.wait_send())
        crossing(j, lambda copy, s: copy.wait_send())
        return carry

    lax.fori_loop(0, last, drain, 0)
    for i in range(1, count):
        for m in range(3):
            weight_out(m, i).wait_send()
            weight_over(m, i).wait_send()
    for i in range(1, count):
        decay_copy(i).wait_send()
    own_result().wait()
    for i in range(1, count):
        result((me + i) % count).wait_send()
        result_in(i).wait_recv()


def all_remote(inner, tokens, w_query, w_key, w_value, norm_gain, log_decay, lengths):
    rows_here, width = tokens.shape
    heads_here, depth, size = w_query.shape
    count = lax.axis_size("seq")
    mine = heads_here // count
    outer = count // inner
    columns = 3 * mine * size
    anywhere = pl.BlockSpec(memory_space=pl.ANY)
    dma = pltpu.SemaphoreType.DMA
    return pl.pallas_call(
        functools.partial(gather_kernel, inner, lengths.shape[0]),
        out_shape=jax.ShapeDtypeStruct((rows_here, heads_here * size), BF16),
        in_specs=[pl.BlockSpec(memory_space=pltpu.SMEM)]
        + [anywhere] * 4
        + [pl.BlockSpec(memory_space=pltpu.VMEM)] * 2,
        out_specs=anywhere,
        scratch_shapes=[
            pltpu.VMEM((count, 2, rows_here // 2, width), BF16),
            pltpu.VMEM((3, mine, width, size), BF16),
            pltpu.VMEM((width, columns), BF16),
            pltpu.VMEM((rows_here * count, columns), BF16),
            pltpu.VMEM((count, rows_here, mine * size), BF16),
            pltpu.VMEM((count, heads_here, rows_here), BF16),
            pltpu.VMEM((count, rows_here // BLOCK, heads_here, BLOCK), F32),
            pltpu.VMEM((mine, size, size), F32),
            dma((2,)),
            dma((3,)),
            dma((2, 2 * outer)),
            dma((inner, 2 * outer)),
            dma((inner, 2 * outer)),
            dma((count, 2)),
            dma((2, count, 3)),
            dma((2, count, 3)),
            dma((count,)),
            dma((count,)),
            dma((count,)),
            dma((count,)),
        ],
        compiler_params=pltpu.CompilerParams(
            collective_id=0, has_side_effects=True, vmem_limit_bytes=56 * 2**20
        ),
    )(lengths, tokens, w_query, w_key, w_value, log_decay, norm_gain)


def project_plain(tokens, w_query, w_key, w_value):
    rows_here, width = tokens.shape
    heads_here, depth, size = w_query.shape
    mine = heads_here // lax.axis_size("seq")
    part = width // lax.axis_size("head")
    half = lax.dynamic_slice(tokens, (0, lax.axis_index("head") * part), (rows_here, part))
    gathered = lax.all_gather(half, "seq", axis=0, tiled=True)
    everyone = lax.all_gather(gathered, "head", axis=1, tiled=True)
    stacked = jnp.stack([w_query, w_key, w_value])
    moved = lax.all_to_all(stacked, "seq", split_axis=1, concat_axis=2, tiled=True)
    weights = jnp.transpose(moved, (2, 0, 1, 3)).reshape(width, 3 * mine * size)
    return jnp.dot(everyone, weights, preferred_element_type=F32).astype(BF16)


def body(tokens, w_query, w_key, w_value, norm_gain, log_decay, lengths):
    rows_here, width = tokens.shape
    heads_here, depth, size = w_query.shape
    count = lax.axis_size("seq")
    mine = heads_here // count
    total = rows_here * count
    fits = 2 * (total * width + total * 3 * mine * size + 6 * mine * size * width) < 48 * 2**20
    if fits and lax.axis_size("groups") % 2 == 0 and lax.axis_size("head") == 2:
        inner = 2 if count % 2 == 0 else 1
        out = all_remote(inner, tokens, w_query, w_key, w_value, norm_gain, log_decay, lengths)
        return out.reshape(rows_here, heads_here, size)
    qkv = project_plain(tokens, w_query, w_key, w_value)
    decays = lax.all_gather(log_decay, "seq", axis=1, tiled=True)
    first_head = lax.axis_index("seq") * mine
    decays = lax.dynamic_slice_in_dim(decays, first_head, mine, axis=0)
    gains = lax.dynamic_slice_in_dim(norm_gain, first_head, mine, axis=0)
    out = pl.pallas_call(
        functools.partial(attend_kernel, lengths.shape[0]),
        grid=(count,),
        out_shape=jax.ShapeDtypeStruct((total, mine * size), BF16),
        in_specs=[
            pl.BlockSpec(memory_space=pltpu.SMEM),
            pl.BlockSpec((rows_here, 3 * mine * size), lambda i: (i, 0)),
            pl.BlockSpec((mine, rows_here), lambda i: (0, i)),
            pl.BlockSpec((mine, size), lambda i: (0, 0)),
        ],
        out_specs=pl.BlockSpec((rows_here, mine * size), lambda i: (i, 0)),
        scratch_shapes=[pltpu.VMEM((mine, size, size), F32)],
        compiler_params=pltpu.CompilerParams(vmem_limit_bytes=32 * 2**20),
    )(lengths, qkv, decays, gains)
    back = lax.all_to_all(out, "seq", split_axis=0, concat_axis=1, tiled=True)
    return back.reshape(rows_here, heads_here, size)


def solution(mesh):
    return jax.shard_map(
        body,
        mesh=mesh,
        in_specs=(
            P(("groups", "seq"), None),
            P("head", "seq", None),
            P("head", "seq", None),
            P("head", "seq", None),
            P("head", None),
            P("head", ("groups", "seq")),
            P("groups"),
        ),
        out_specs=P(("groups", "seq"), "head", None),
        check_vma=False,
    )
```

```python
import functools

import jax
import jax.numpy as jnp
from jax import lax
from jax.experimental import pallas as pl
from jax.experimental.pallas import tpu as pltpu
from jax.sharding import PartitionSpec as P

BLOCK = 128
NT = (((1,), (1,)), ((), ()))
TN = (((0,), (0,)), ((), ()))
F32 = jnp.float32
BF16 = jnp.bfloat16
MESH = pl.DeviceIdType.MESH


def attend_block(q, k, v, decay, seg, state, gain, consts):
    lower, upper, above = consts
    visible, entered, leaves, passes = seg
    size = q.shape[0]
    rows = jnp.broadcast_to(decay, (size, size))
    gap = lax.dot_general(lower, jnp.where(above, rows, 0), NT, preferred_element_type=F32)
    running = lax.dot_general(lower, rows, NT, preferred_element_type=F32)
    rest = lax.dot_general(upper, rows, NT, preferred_element_type=F32)
    scores = lax.dot_general(q, k, NT, preferred_element_type=F32)
    weights = (scores * jnp.where(visible, jnp.exp(gap), 0.0)).astype(BF16)
    intra = jnp.dot(weights, v, preferred_element_type=F32)
    enter = jnp.where(entered, 0.0, jnp.exp(running))
    carried = jnp.dot(q, state.astype(BF16), preferred_element_type=F32)
    attended = intra + enter * carried
    inv = lax.rsqrt(jnp.mean(attended * attended, axis=1, keepdims=True) + 1e-06)
    out = (attended * inv * gain).astype(BF16)
    carry = jnp.where(leaves, 0.0, jnp.exp(rest))
    weighted = (k.astype(F32) * carry).astype(BF16)
    update = lax.dot_general(weighted, v, TN, preferred_element_type=F32)
    keep = jnp.where(passes, jnp.exp(running[size - 1 : size, :]), 0.0)
    return out, keep * state + update


def segment_of(position, lens_ref, base, prompts):
    end = jnp.int32(0)
    total = 0 * position
    for j in range(prompts):
        end = end + lens_ref[base + j]
        total = total + jnp.where(position >= end, 1, 0)
    return total


def attend_shard(step, rows, heads, lens_ref, prompts, part, decay, gain, state_ref, store):
    ti = lax.broadcasted_iota(jnp.int32, (BLOCK, BLOCK), 0)
    si = lax.broadcasted_iota(jnp.int32, (BLOCK, BLOCK), 1)
    consts = ((ti >= si).astype(F32).astype(BF16), (ti < si).astype(F32).astype(BF16), ti < si)
    for b in range(rows // BLOCK):
        first = (step * rows + b * BLOCK).astype(jnp.int32)
        seg_t = segment_of(first + ti, lens_ref, 0, prompts)
        seg_s = segment_of(first + si, lens_ref, 0, prompts)
        seg_before = segment_of(first - 1, lens_ref, 0, prompts)
        seg_last = segment_of(first + BLOCK - 1, lens_ref, 0, prompts)
        seg_before = jnp.where(first == 0, -1, seg_before)
        seg = (
            (ti >= si) & (seg_t == seg_s),
            seg_t != seg_before,
            seg_t != seg_last,
            seg_before == seg_last,
        )
        for h in range(heads):
            out, state = attend_block(
                *part(b, h), decay(b, h), seg, state_ref[h], gain(h), consts
            )
            state_ref[h] = state
            store(b, h, out)


def attend_kernel(prompts, lens_ref, qkv_ref, ld_ref, gain_ref, out_ref, state_ref):
    step = pl.program_id(0)
    heads = ld_ref.shape[0]
    size = gain_ref.shape[1]

    @pl.when(step == 0)
    def _():
        state_ref[...] = jnp.zeros_like(state_ref)

    def here(b):
        return slice(b * BLOCK, (b + 1) * BLOCK)

    def part(b, h):
        return [qkv_ref[here(b), (i * heads + h) * size : (i * heads + h + 1) * size] for i in range(3)]

    def store(b, h, out):
        out_ref[here(b), h * size : (h + 1) * size] = out

    attend_shard(
        step, qkv_ref.shape[0], heads, lens_ref, prompts, part,
        lambda b, h: ld_ref[h : h + 1, here(b)], lambda h: gain_ref[h : h + 1, :], state_ref, store,
    )


def gather_kernel(
    inner, prompts, lens_ref, tok_hbm, wq, wk, wv, ld_ref, gain_ref, out_hbm,
    tok, landed, joined, qkv, ready, decays, wide, state_ref,
    own_sem, w_own, z_send, y_send, core_send, tok_recv, w_send, w_recv, d_send, d_recv, o_send, o_recv,
):
    count = lax.axis_size("seq")
    outer = count // inner
    me, core, group = lax.axis_index("seq"), lax.axis_index("head"), lax.axis_index("groups")
    far, near = me // inner, me % inner
    weights = (wq, wk, wv)
    mine, depth = wq.shape[0] // count, wq.shape[1]
    part = depth // 2
    side = group % 2
    rows = tok.shape[2]
    size = wq.shape[2]
    other_core = {"head": 1 - core}
    twin = {"groups": group + 1 - 2 * side}

    barrier = pltpu.get_barrier_semaphore()
    for i in range(1, count):
        pl.semaphore_signal(barrier, device_id={"seq": (me + i) % count}, device_id_type=MESH)
    pl.semaphore_signal(barrier, device_id=other_core, device_id_type=MESH)
    pl.semaphore_signal(barrier, device_id=twin, device_id_type=MESH)
    pl.semaphore_wait(barrier, count + 1)

    def own_copy(h):
        return pltpu.make_async_copy(tok_hbm.at[pl.ds(h * rows, rows)], tok.at[me, h], own_sem.at[h])

    def own_weights(m):
        return pltpu.make_async_copy(
            weights[m].at[pl.ds(me * mine, mine)],
            landed.at[m, :, pl.ds(pl.multiple_of(me * depth, 16), depth)],
            w_own.at[m],
        )

    def remote(src, dst, send, recv, device):
        return pltpu.make_async_remote_copy(
            src_ref=src, dst_ref=dst, send_sem=send, recv_sem=recv, device_id=device, device_id_type=MESH
        )

    def shard(s, h, send, device):
        return remote(tok.at[s, h], tok.at[s, h], send, tok_recv.at[s, h], device)

    def slot(m, s, half):
        start = pl.multiple_of(s * depth + half * part, 16)
        return landed.at[m, :, pl.ds(start, part)]

    def weight_out(m, i):
        to = (me + i) % count
        src = weights[m].at[pl.ds(to * mine, mine), pl.ds(pl.multiple_of(side * part, 16), part)]
        return remote(src, slot(m, me, side), w_send.at[0, i, m], w_recv.at[side, me, m], {"seq": to})

    def weight_over(m, i):
        s = (me + count - i) % count
        return remote(slot(m, s, side), slot(m, s, side), w_send.at[1, i, m], w_recv.at[side, s, m], twin)

    def weight_in(m, i, half):
        s = (me + count - i) % count
        return remote(slot(m, s, half), slot(m, s, half), w_send.at[1, i, m], w_recv.at[half, s, m], twin)

    def decay_copy(i):
        src = decays.at[me]
        return remote(src, src, d_send.at[i], d_recv.at[me], {"seq": (me + i) % count})

    def decay_in(i):
        s = (me + i) % count
        return remote(decays.at[s], decays.at[s], d_send.at[i], d_recv.at[s], {"seq": s})

    def columns_of(s):
        return pl.ds(pl.multiple_of(s * (mine * size), 128), mine * size)

    def result(s):
        return remote(ready.at[s], out_hbm.at[:, columns_of(me)], o_send.at[s], o_recv.at[me], {"seq": s})

    def result_in(i):
        s = (me + i) % count
        return remote(ready.at[s], out_hbm.at[:, columns_of(s)], o_send.at[s], o_recv.at[s], {"seq": s})

    def own_result():
        return pltpu.make_async_copy(ready.at[me], out_hbm.at[:, columns_of(me)], o_recv.at[me])

    for h in range(2):
        own_copy(h).start()
    decays[me] = ld_ref[...]
    for m in range(3):
        own_weights(m).start()
    for h in range(2):
        own_copy(h).wait()

    def forwards(j, act):
        step = (j + 1) // 2
        offset = jnp.where(j % 2 == 1, -step, step)
        place = far + offset
        s = place * inner + near
        inside = (place >= 0) & (place < outer)

        @pl.when(inside & (offset <= 0) & (far + 1 < outer))
        def _():
            act(shard(s, core, z_send.at[0, j], {"seq": me + inner}))

        @pl.when(inside & (offset >= 0) & (far > 0))
        def _():
            act(shard(s, core, z_send.at[1, j], {"seq": me - inner}))

        for k in range(1, inner):
            @pl.when(inside)
            def _():
                act(shard(s, core, y_send.at[k, j], {"seq": far * inner + (near + k) % inner}))

        @pl.when(inside & (j > 0))
        def _():
            act(shard(s, core, core_send.at[0, j], other_core))

    def crossing(j, act):
        step = (j + 1) // 2
        place = far + jnp.where(j % 2 == 1, -step, step)
        for k in range(1, inner):
            s = place * inner + (near + k) % inner

            @pl.when((place >= 0) & (place < outer))
            def _():
                act(shard(s, core, core_send.at[k, j], other_core), s)

    def arrived(s, h):
        shard(s, h, own_sem.at[0], other_core).wait_recv()

    def receive_and_start(copy, s):
        arrived(s, core)
        copy.start()

    forwards(0, lambda copy: copy.start())
    for i in range(1, count):
        for m in range(3):
            weight_out(m, i).start()
    for i in range(1, count):
        decay_copy(i).start()

    last = 2 * outer - 1

    def serve(j, carry):
        step = (j + 1) // 2
        place = far + jnp.where(j % 2 == 1, -step, step)

        @pl.when((j < last) & (place >= 0) & (place < outer))
        def _():
            arrived(place * inner + near, core)

        @pl.when(j < last)
        def _():
            forwards(j, lambda copy: copy.start())

        @pl.when(j >= 2)
        def _():
            crossing(j - 2, receive_and_start)

        @pl.when(j == 2)
        def _():
            for i in range(1, count):
                for m in range(3):
                    weight_in(m, i, side).wait_recv()
                    weight_over(m, i).start()

        return carry

    lax.fori_loop(1, last, serve, 0)

    for m in range(3):
        own_weights(m).wait()
    for i in range(1, count):
        for m in range(3):
            weight_in(m, i, 1 - side).wait_recv()

    def join(s, carry):
        here = pl.ds(pl.multiple_of(s * depth, 16), depth)
        for m in range(3):
            for h in range(mine):
                at = (m * mine + h) * size
                joined[here, at : at + size] = landed[m, h, here, :]
        return carry

    lax.fori_loop(0, count, join, 0)

    def project(j, carry):
        step = (j + 1) // 2
        place = far + jnp.where(j % 2 == 1, -step, step)

        @pl.when((j >= last - 2) & (place >= 0) & (place < outer))
        def _():
            for k in range(1, inner):
                s = place * inner + (near + k) % inner
                receive_and_start(shard(s, core, core_send.at[k, j], other_core), s)

        @pl.when((place >= 0) & (place < outer))
        def _():
            def one(k, carry):
                s = place * inner + (near + k) % inner

                @pl.when(s != me)
                def _():
                    arrived(s, 1 - core)

                for h in range(2):
                    start = pl.multiple_of((2 * s + h) * rows, 16)
                    qkv[pl.ds(start, rows), :] = jnp.dot(
                        tok[s, h], joined[...], preferred_element_type=F32
                    ).astype(BF16)
                return carry

            lax.fori_loop(0, inner, one, 0)

        return carry

    lax.fori_loop(0, last, project, 0)

    for i in range(1, count):
        decay_in(i).wait_recv()
    for b in range(wide.shape[1]):
        wide[:, b] = decays[:, :, b * BLOCK : (b + 1) * BLOCK].astype(F32)
    state_ref[...] = jnp.zeros_like(state_ref)
    row_count = 2 * rows

    def attend(s, carry):
        def part(b, h):
            here = pl.ds(pl.multiple_of(s * row_count + b * BLOCK, BLOCK), BLOCK)
            return [qkv[here, (i * mine + h) * size : (i * mine + h + 1) * size] for i in range(3)]

        def decay(b, h):
            return wide[s, b, pl.ds(me * mine + h, 1), :].astype(BF16)

        def store(b, h, out):
            ready[s, b * BLOCK : (b + 1) * BLOCK, h * size : (h + 1) * size] = out

        attend_shard(
            s, row_count, mine, lens_ref, prompts, part, decay,
            lambda h: gain_ref[pl.ds(me * mine + h, 1), :], state_ref, store,
        )

        @pl.when(s != me)
        def _():
            result(s).start()

        @pl.when(s == me)
        def _():
            own_result().start()

        return carry

    lax.fori_loop(0, count, attend, 0)

    def drain(j, carry):
        forwards(j, lambda copy: copy.wait_send())
        crossing(j, lambda copy, s: copy.wait_send())
        return carry

    lax.fori_loop(0, last, drain, 0)
    for i in range(1, count):
        for m in range(3):
            weight_out(m, i).wait_send()
            weight_over(m, i).wait_send()
    for i in range(1, count):
        decay_copy(i).wait_send()
    own_result().wait()
    for i in range(1, count):
        result((me + i) % count).wait_send()
        result_in(i).wait_recv()


def all_remote(inner, tokens, w_query, w_key, w_value, norm_gain, log_decay, lengths):
    rows_here, width = tokens.shape
    heads_here, depth, size = w_query.shape
    count = lax.axis_size("seq")
    mine = heads_here // count
    outer = count // inner
    columns = 3 * mine * size
    anywhere = pl.BlockSpec(memory_space=pl.ANY)
    dma = pltpu.SemaphoreType.DMA
    return pl.pallas_call(
        functools.partial(gather_kernel, inner, lengths.shape[0]),
        out_shape=jax.ShapeDtypeStruct((rows_here, heads_here * size), BF16),
        in_specs=[pl.BlockSpec(memory_space=pltpu.SMEM)]
        + [anywhere] * 4
        + [pl.BlockSpec(memory_space=pltpu.VMEM)] * 2,
        out_specs=anywhere,
        scratch_shapes=[
            pltpu.VMEM((count, 2, rows_here // 2, width), BF16),
            pltpu.VMEM((3, mine, width, size), BF16),
            pltpu.VMEM((width, columns), BF16),
            pltpu.VMEM((rows_here * count, columns), BF16),
            pltpu.VMEM((count, rows_here, mine * size), BF16),
            pltpu.VMEM((count, heads_here, rows_here), BF16),
            pltpu.VMEM((count, rows_here // BLOCK, heads_here, BLOCK), F32),
            pltpu.VMEM((mine, size, size), F32),
            dma((2,)),
            dma((3,)),
            dma((2, 2 * outer)),
            dma((inner, 2 * outer)),
            dma((inner, 2 * outer)),
            dma((count, 2)),
            dma((2, count, 3)),
            dma((2, count, 3)),
            dma((count,)),
            dma((count,)),
            dma((count,)),
            dma((count,)),
        ],
        compiler_params=pltpu.CompilerParams(
            collective_id=0, has_side_effects=True, vmem_limit_bytes=56 * 2**20
        ),
    )(lengths, tokens, w_query, w_key, w_value, log_decay, norm_gain)


def project_plain(tokens, w_query, w_key, w_value):
    rows_here, width = tokens.shape
    heads_here, depth, size = w_query.shape
    mine = heads_here // lax.axis_size("seq")
    part = width // lax.axis_size("head")
    half = lax.dynamic_slice(tokens, (0, lax.axis_index("head") * part), (rows_here, part))
    gathered = lax.all_gather(half, "seq", axis=0, tiled=True)
    everyone = lax.all_gather(gathered, "head", axis=1, tiled=True)
    stacked = jnp.stack([w_query, w_key, w_value])
    moved = lax.all_to_all(stacked, "seq", split_axis=1, concat_axis=2, tiled=True)
    weights = jnp.transpose(moved, (2, 0, 1, 3)).reshape(width, 3 * mine * size)
    return jnp.dot(everyone, weights, preferred_element_type=F32).astype(BF16)


def body(tokens, w_query, w_key, w_value, norm_gain, log_decay, lengths):
    rows_here, width = tokens.shape
    heads_here, depth, size = w_query.shape
    count = lax.axis_size("seq")
    mine = heads_here // count
    total = rows_here * count
    fits = 2 * (total * width + total * 3 * mine * size + 6 * mine * size * width) < 48 * 2**20
    if fits and lax.axis_size("groups") % 2 == 0 and lax.axis_size("head") == 2:
        inner = 2 if count % 2 == 0 else 1
        out = all_remote(inner, tokens, w_query, w_key, w_value, norm_gain, log_decay, lengths)
        return out.reshape(rows_here, heads_here, size)
    qkv = project_plain(tokens, w_query, w_key, w_value)
    decays = lax.all_gather(log_decay, "seq", axis=1, tiled=True)
    first_head = lax.axis_index("seq") * mine
    decays = lax.dynamic_slice_in_dim(decays, first_head, mine, axis=0)
    gains = lax.dynamic_slice_in_dim(norm_gain, first_head, mine, axis=0)
    out = pl.pallas_call(
        functools.partial(attend_kernel, lengths.shape[0]),
        grid=(count,),
        out_shape=jax.ShapeDtypeStruct((total, mine * size), BF16),
        in_specs=[
            pl.BlockSpec(memory_space=pltpu.SMEM),
            pl.BlockSpec((rows_here, 3 * mine * size), lambda i: (i, 0)),
            pl.BlockSpec((mine, rows_here), lambda i: (0, i)),
            pl.BlockSpec((mine, size), lambda i: (0, 0)),
        ],
        out_specs=pl.BlockSpec((rows_here, mine * size), lambda i: (i, 0)),
        scratch_shapes=[pltpu.VMEM((mine, size, size), F32)],
        compiler_params=pltpu.CompilerParams(vmem_limit_bytes=32 * 2**20),
    )(lengths, qkv, decays, gains)
    back = lax.all_to_all(out, "seq", split_axis=0, concat_axis=1, tiled=True)
    return back.reshape(rows_here, heads_here, size)


def solution(mesh):
    return jax.shard_map(
        body,
        mesh=mesh,
        in_specs=(
            P(("groups", "seq"), None),
            P("head", "seq", None),
            P("head", "seq", None),
            P("head", "seq", None),
            P("head", None),
            P("head", ("groups", "seq")),
            P("groups"),
        ),
        out_specs=P(("groups", "seq"), "head", None),
        check_vma=False,
    )
```
